256 devices in a mesh: dp: 32 (over x_hi, z, core), tensor: 8 (over y, x_lo).
Axes of the slice: x: 4 (x_hi: 2, x_lo: 2; x = x_hi * 2 + x_lo), y: 4, z: 8, core: 2. Of those that a mesh axis runs over, the one named last changes fastest.
Arguments:
- hidden: bfloat16 [65536, 14336], P('dp', 'tensor'), may hold values from -6 to 6
- grad_out: bfloat16 [65536, 4096], P(('dp', 'tensor')), may hold values from -6 to 6
- proj_in: bfloat16 [64, 14336], P(None, 'tensor'), may hold values from -0.046875 to 0.046875
- proj_out: bfloat16 [64, 4096], replicated, may hold values from -0.09375 to 0.09375
- queries: bfloat16 [4096, 4096], P(('dp', 'tensor')), may hold values from -6 to 6
Outputs:
- scores: float32 [4096, 512], P(('dp', 'tensor'))
The draws below stay inside these ranges and needn't reach their ends.
All inputs are finite; a program needn't handle non-finite values.
Results may differ from the reference program's by a relative error of at most 0.0041.
Values may be sent and summed in bfloat16 or wider, within the bound.
A program may use at most 64 MiB of HBM per device.

```python
import jax
import jax.numpy as jnp
from jax import lax

D = 4096
FF = 14336
RANK = 64
SEQ = 128
TOKENS = 65536
NQ = 4096


def level_of(key, dims, pieces, low, largest):
    level, own = 1.0, jax.random.fold_in(key, 6)
    for position, parts in pieces:
        steps = jnp.exp(jax.random.uniform(jax.random.fold_in(own, position), (parts,), jnp.float32, low / len(pieces), largest / len(pieces)))
        level = level * jnp.repeat(steps, dims[position] // parts).reshape([-1 if axis == position else 1 for axis in range(len(dims))])
    return level


def bell_draw(own_key, extent, spread, bound, cuts=(), held_as=jnp.bfloat16):
    result = spread * jax.random.normal(own_key, extent, jnp.float32)
    if cuts:
        result = result * level_of(own_key, extent, cuts, -0.22, 0.18)
    return jnp.clip(result, -bound, bound).astype(held_as)


def setup_inputs(seed: int = 0) -> dict:
    streams_of = jax.random.split(jax.random.key(seed), 6)
    hidden = bell_draw(streams_of[0], (TOKENS, FF), 1.0, 6.0, ((0, 32), (1, 8)))
    grad_out = bell_draw(streams_of[1], (TOKENS, D), 1.0, 6.0, ((0, 256),))
    proj_in = bell_draw(streams_of[2], (RANK, FF), FF ** -0.5, 0.046875, ((1, 8),))
    proj_out = bell_draw(streams_of[3], (RANK, D), D ** -0.5, 0.09375)
    queries = bell_draw(streams_of[4], (NQ, RANK * RANK), 1.0, 6.0, ((0, 256),))
    return {"hidden": hidden, "grad_out": grad_out, "proj_in": proj_in, "proj_out": proj_out, "queries": queries}


def reference(hidden, grad_out, proj_in, proj_out, queries):
    projected_in = jnp.dot(hidden, proj_in.T, preferred_element_type=jnp.float32)
    projected_out = jnp.dot(grad_out, proj_out.T, preferred_element_type=jnp.float32).astype(jnp.bfloat16)
    sequences = projected_in.shape[0] // SEQ
    outer_sums = jnp.einsum("sti,stj->sij", projected_in.reshape(sequences, SEQ, RANK), projected_out.astype(jnp.float32).reshape(sequences, SEQ, RANK), precision=lax.Precision.HIGHEST).reshape(sequences, RANK * RANK)
    features = (outer_sums * (SEQ ** -0.5)).astype(jnp.bfloat16)
    return jnp.dot(queries, features.T, preferred_element_type=jnp.float32) * (1.0 / RANK)
```

```python
import functools

import jax
import jax.numpy as jnp
from jax import lax
from jax.experimental import pallas as pl
from jax.experimental.pallas import tpu as pltpu
from jax.sharding import PartitionSpec as P

MESH = pl.DeviceIdType.MESH
BF16, F32 = jnp.bfloat16, jnp.float32
SEQ = 128
RANK = 64
LANES = 128
HALF = RANK // 2

ORDER = (5, 4, 3, 7, 2, 6, 1, 0)


def flip(value, mask, bits):
    result = 0
    for bit in range(bits):
        digit = lax.rem(lax.div(value, 1 << bit), 2)
        result = result + (1 << bit) * (1 - digit if (mask >> bit) & 1 else digit)
    return result


def dot_nt(a, b):
    return lax.dot_general(a, b, (((1,), (1,)), ((), ())), preferred_element_type=F32)


def dot_nn(a, b):
    return lax.dot_general(a, b, (((1,), (0,)), ((), ())), preferred_element_type=F32)


def pack_pair(block):
    return jnp.concatenate([block[:SEQ], block[SEQ:]], axis=1)


def kernel(
    hidden, grad_out, proj_in, proj_out, queries, out,
    x_v, g_v, wi_v, wo_v, q_v, rs_send, rs_recv, r_v, f_send, f_recv, feats, s_send, s_recv, perm,
    x_sem, w_sem, rs_ss, rs_rs, q_ss, q_rs, qc_ss, qc_rs, f_ss, f_rs, s_ss, s_rs,
):
    dp, t = lax.axis_index("dp"), lax.axis_index("tensor")
    c, z, xh = lax.rem(dp, 2), lax.rem(lax.div(dp, 2), 8), lax.div(dp, 16)

    def tc_peer(b, k):
        return (dp + 1 - 2 * c if b else dp, flip(t, k, 3))

    def xz_peer(dx, dz):
        x = 1 - xh if dx else xh
        return ((x * 8 + lax.rem(z + dz, 8)) * 2 + c, t)

    tc_all = [(b, k) for b in (0, 1) for k in range(8) if b or k]
    xz_all = [(dx, dz) for dx in (0, 1) for dz in range(8) if dx or dz]

    loads = [pltpu.make_async_copy(proj_in, wi_v, w_sem.at[0])]
    blocks = {}
    for k in ORDER:
        rows = pl.ds(pl.multiple_of(flip(t, k, 3) * 256, 256), 256)
        blocks[k] = pltpu.make_async_copy(hidden.at[rows], x_v.at[k], x_sem.at[k])
    load_wo = pltpu.make_async_copy(proj_out, wo_v, w_sem.at[1])
    load_g = pltpu.make_async_copy(grad_out, g_v, w_sem.at[2])
    load_q = pltpu.make_async_copy(queries, q_v.at[0], w_sem.at[3])
    loads[0].start()
    for k in ORDER:
        blocks[k].start()
    load_wo.start()
    load_g.start()
    load_q.start()

    barrier = pltpu.get_barrier_semaphore()
    for b, k in tc_all:
        pl.semaphore_signal(barrier, inc=1, device_id=tc_peer(b, k), device_id_type=MESH)
    for dx, dz in xz_all:
        pl.semaphore_signal(barrier, inc=1, device_id=xz_peer(dx, dz), device_id_type=MESH)
    pl.semaphore_wait(barrier, len(tc_all) + len(xz_all))

    def remote(src, dst, ss, rs, peer):
        return pltpu.make_async_remote_copy(
            src_ref=src, dst_ref=dst, send_sem=ss, recv_sem=rs, device_id=peer, device_id_type=MESH
        )

    loads[0].wait()
    wi = wi_v[...]
    rs = {}
    own = None
    for k in ORDER:
        blocks[k].wait()
        part = pack_pair(dot_nt(x_v[k], wi))
        if k:
            rs_send[k] = part.astype(BF16)
            rs[k] = remote(rs_send.at[k], rs_recv.at[k], rs_ss.at[k], rs_rs.at[k], tc_peer(0, k))
            rs[k].start()
        else:
            own = part

    load_q.wait()
    qs = {}
    for k in ORDER[:-1]:
        qs[k] = remote(q_v.at[0], q_v.at[k], q_ss.at[k], q_rs.at[k], tc_peer(0, k))
        qs[k].start()
    qc = {0: remote(q_v.at[0], q_v.at[8], qc_ss.at[0], qc_rs.at[0], tc_peer(1, 0))}
    qc[0].start()

    load_wo.wait()
    load_g.wait()
    pout = pack_pair(dot_nt(g_v[...], wo_v[...])).astype(BF16)

    row = lax.broadcasted_iota(jnp.int32, (512, LANES), 0)
    lane = lax.broadcasted_iota(jnp.int32, (512, LANES), 1)
    b_, a_, tl_ = row // 256, (row // 128) % 2, (row // 32) % 4
    dx_, dz_, s_ = (row // 16) % 2, (row // 2) % 8, row % 2
    src_c = (c + b_) % 2
    src_t = (((t // 4) + a_) % 2) * 4 + tl_
    src_xz = ((xh + dx_) % 2) * 8 + (z - dz_ + 8) % 8
    target = src_xz * 32 + src_c * 16 + src_t * 2 + s_
    for block in range(4):
        perm[:, block * LANES : (block + 1) * LANES] = jnp.where(
            target == lane + block * LANES, 1.0, 0.0
        ).astype(BF16)

    total = own
    for k in ORDER[:-1]:
        rs[k].wait_recv()
        total = total + rs_recv[k].astype(F32)
    pin = total.T
    hi = pin.astype(BF16)
    lo = (pin - hi.astype(F32)).astype(BF16)
    r_v[...] = (dot_nn(hi, pout) + dot_nn(lo, pout)) * (SEQ ** -0.5)
    left = lax.broadcasted_iota(jnp.int32, (HALF, LANES), 1) < RANK
    even, odd = r_v[pl.ds(0, HALF, stride=2), :], r_v[pl.ds(1, HALF, stride=2), :]
    f0 = jnp.where(left, even, pltpu.roll(odd, RANK, 1))
    even, odd = r_v[pl.ds(RANK, HALF, stride=2), :], r_v[pl.ds(RANK + 1, HALF, stride=2), :]
    f1 = jnp.where(left, pltpu.roll(even, RANK, 1), odd)
    mine = jnp.concatenate([f0, f1], axis=0).astype(BF16)
    f_send[...] = mine

    fs = {}
    for dx, dz in sorted(xz_all, key=lambda o: -(2 * o[0] + min(o[1], 8 - o[1]))):
        slot = dx * 8 + dz
        fs[slot] = remote(f_send, f_recv.at[slot], f_ss.at[slot], f_rs.at[slot], xz_peer(dx, dz))
        fs[slot].start()

    for k in ORDER[:-1][::-1]:
        qs[k].wait_recv()
        qc[k] = remote(q_v.at[k], q_v.at[8 + k], qc_ss.at[k], qc_rs.at[k], tc_peer(1, 0))
        qc[k].start()

    def spread(slot, block):
        both = block.astype(F32)
        for s in range(2):
            feats[pl.ds(slot * 2 + s, HALF, stride=32), :] = both[s * HALF : (s + 1) * HALF]

    spread(0, mine)
    for slot in list(fs)[::-1]:
        fs[slot].wait_recv()
        spread(slot, f_recv[slot])
    for k in range(8):
        qc[k].wait_recv()

    right = jnp.concatenate(
        [feats[i * 32 : (i + 1) * 32, :].astype(BF16) for i in range(HALF)], axis=1
    )
    scores = dot_nt(q_v[...].reshape(256, 4096), right) * (1.0 / RANK)
    scores = jnp.concatenate([scores, jnp.zeros((256, LANES - 32), F32)], axis=1)
    scores = pltpu.roll(scores, lax.rem(t, 4) * 32, 1)
    s_send[...] = scores.reshape(16, 16, LANES)

    ssd = {}
    for b, k in [(b, k) for k in ORDER for b in (1, 0) if b or k]:
        slot = b * 8 + k
        ssd[slot] = remote(s_send.at[slot], s_recv.at[slot], s_ss.at[slot], s_rs.at[slot], tc_peer(b, k))
        ssd[slot].start()
    for slot in ssd:
        ssd[slot].wait_recv()
    groups = []
    for g in range(4):
        acc = None
        for j in range(4):
            slot = g * 4 + j
            block = s_recv[slot] if slot else s_send[0]
            acc = block if acc is None else acc + block
        groups.append(acc)
    wide = jnp.concatenate(groups, axis=1)
    p1 = wide.astype(BF16)
    rest = wide - p1.astype(F32)
    p2 = rest.astype(BF16)
    p3 = (rest - p2.astype(F32)).astype(BF16)
    placed = dot_nn(jnp.concatenate([p1, p2, p3], axis=0), perm[...])
    out[...] = (placed[:16] + placed[16:32]) + placed[32:]

    for sends in (rs, qs, qc, fs, ssd):
        for copy in sends.values():
            copy.wait_send()


def body(hidden, grad_out, proj_in, proj_out, queries):
    dma = pltpu.SemaphoreType.DMA
    scratch = [
        pltpu.VMEM((8, 256, 1792), BF16),
        pltpu.VMEM((256, 4096), BF16),
        pltpu.VMEM((64, 1792), BF16),
        pltpu.VMEM((64, 4096), BF16),
        pltpu.VMEM((16, 16, 4096), BF16),
        pltpu.VMEM((8, SEQ, LANES), BF16),
        pltpu.VMEM((8, SEQ, LANES), BF16),
        pltpu.VMEM((LANES, LANES), F32),
        pltpu.VMEM((RANK, LANES), BF16),
        pltpu.VMEM((16, RANK, LANES), BF16),
        pltpu.VMEM((HALF * 32, LANES), F32),
        pltpu.VMEM((16, 16, LANES), F32),
        pltpu.VMEM((16, 16, LANES), F32),
        pltpu.VMEM((512, 512), BF16),
        dma((8,)), dma((4,)), dma((8,)), dma((8,)), dma((8,)), dma((8,)),
        dma((8,)), dma((8,)), dma((16,)), dma((16,)), dma((16,)), dma((16,)),
    ]
    return pl.pallas_call(
        kernel,
        out_shape=jax.ShapeDtypeStruct((16, 512), F32),
        in_specs=[pl.BlockSpec(memory_space=pltpu.HBM)] * 5,
        out_specs=pl.BlockSpec(memory_space=pltpu.VMEM),
        scratch_shapes=scratch,
        compiler_params=pltpu.CompilerParams(
            collective_id=0, has_side_effects=True, vmem_limit_bytes=40 << 20
        ),
    )(hidden, grad_out, proj_in, proj_out, queries)


def solution(mesh):
    placed = (
        P("dp", "tensor"),
        P(("dp", "tensor"), None),
        P(None, "tensor"),
        P(),
        P(("dp", "tensor"), None),
    )
    return jax.shard_map(
        body, mesh=mesh, in_specs=placed, out_specs=P(("dp", "tensor"), None), check_vma=False
    )
```

```python
import jax
import jax.numpy as jnp
from jax import lax
from jax.experimental import pallas as pl
from jax.experimental.pallas import tpu as pltpu
from jax.sharding import PartitionSpec as P

MESH = pl.DeviceIdType.MESH
BF16, F32 = jnp.bfloat16, jnp.float32
SEQ = 128
RANK = 64
LANES = 128
FF_PART = 1792
D = 4096
HALF_K = RANK * RANK // 2
TILES = HALF_K // LANES
PITCH = 72

ORDER = (5, 4, 3, 7, 2, 6, 1, 0)
EARLY = 4


def flip(value, mask, bits):
    result = 0
    for bit in range(bits):
        digit = lax.rem(lax.div(value, 1 << bit), 2)
        result = result + (1 << bit) * (1 - digit if (mask >> bit) & 1 else digit)
    return result


def dot_nt(a, b):
    return lax.dot_general(a, b, (((1,), (1,)), ((), ())), preferred_element_type=F32)


def dot_nn(a, b):
    return lax.dot_general(a, b, (((1,), (0,)), ((), ())), preferred_element_type=F32)


def kernel(
    hidden, grad_out, proj_in, proj_out, queries, out,
    x_v, g_v, wi_v, wo_v, q_v, rs_send, rs_recv, r_v, f_send, f_recv, feats, s_send, s_recv, perm,
    x_sem, w_sem, rs_ss, rs_rs, q_ss, q_rs, qc_ss, qc_rs, f_ss, f_rs, s_ss, s_rs,
):
    dp, t = lax.axis_index("dp"), lax.axis_index("tensor")
    c, z, xh = lax.rem(dp, 2), lax.rem(lax.div(dp, 2), 8), lax.div(dp, 16)
    y, xl = lax.div(t, 2), lax.rem(t, 2)
    x = xh * 2 + xl

    def tc_peer(b, k):
        return (dp + 1 - 2 * c if b else dp, flip(t, k, 3))

    def at(px, pz):
        return ((lax.div(px, 2) * 8 + pz) * 2 + c, y * 2 + lax.rem(px, 2))

    def ahead(dx, dz):
        return lax.rem(x + dx, 4), lax.rem(z + dz, 8)

    def behind(dx, dz):
        return lax.rem(x + 4 - dx, 4), lax.rem(z + 8 - dz, 8)

    tc_all = [(b, k) for b in (0, 1) for k in range(8) if b or k]
    xz_all = [(dx, dz) for dx in range(4) for dz in range(8) if dx or dz]
    xz_all.sort(key=lambda o: min(o[0], 4 - o[0]) + min(o[1], 8 - o[1]))

    load_wi = pltpu.make_async_copy(proj_in, wi_v.at[0, pl.ds(0, RANK)], w_sem.at[0])
    load_wi2 = pltpu.make_async_copy(proj_in, wi_v.at[1, pl.ds(RANK, RANK)], w_sem.at[4])
    blocks = {}
    for k in ORDER:
        rows = pl.ds(pl.multiple_of(flip(t, k, 3) * 256, 256), 256)
        blocks[k] = pltpu.make_async_copy(hidden.at[rows], x_v.at[k], x_sem.at[k])
    load_wo = pltpu.make_async_copy(proj_out, wo_v, w_sem.at[1])
    load_g = pltpu.make_async_copy(grad_out, g_v, w_sem.at[2])
    mine_k = pl.ds(pl.multiple_of(xl * HALF_K, HALF_K), HALF_K)
    other_k = pl.ds(pl.multiple_of((1 - xl) * HALF_K, HALF_K), HALF_K)
    load_q = pltpu.make_async_copy(queries.at[:, mine_k], q_v.at[0], w_sem.at[3])
    load_wi.start()
    load_wi2.start()
    for k in ORDER[:2]:
        blocks[k].start()

    with jax.named_scope("greet"):
        barrier = pltpu.get_barrier_semaphore()
        greeted = [tc_peer(b, k) for b, k in tc_all]
        greeted += [at(*ahead(dx, dz)) for dx, dz in xz_all if dz or dx == 2]
        greeted.append(at(lax.rem(x + 3 + 2 * xl, 4), z))
        for peer in greeted[::-1]:
            pl.semaphore_signal(barrier, inc=1, device_id=peer, device_id_type=MESH)

    for k in ORDER[2:]:
        blocks[k].start()
    load_wo.start()
    load_g.start()
    load_q.start()

    def remote(src, dst, ss, rs, peer):
        return pltpu.make_async_remote_copy(
            src_ref=src, dst_ref=dst, send_sem=ss, recv_sem=rs, device_id=peer, device_id_type=MESH
        )

    rs = {}

    def project(k):
        blocks[k].wait()
        return dot_nt(x_v[k, :SEQ], wi_v[0]) + dot_nt(x_v[k, SEQ:], wi_v[1])

    def send_part(k):
        rs[k] = remote(rs_send.at[k], rs_recv.at[k], rs_ss.at[k], rs_rs.at[k], tc_peer(0, k))
        rs[k].start()

    with jax.named_scope("hidden_early"):
        wi_v[0, RANK:, :] = jnp.zeros((RANK, FF_PART), BF16)
        wi_v[1, :RANK, :] = jnp.zeros((RANK, FF_PART), BF16)
        load_wi.wait()
        load_wi2.wait()
        for k in ORDER[:EARLY]:
            rs_send[k] = project(k).astype(BF16)
    with jax.named_scope("entry_wait"):
        pl.semaphore_wait(barrier, len(greeted))
    with jax.named_scope("hidden_late"):
        for k in ORDER[:EARLY]:
            send_part(k)
        for k in ORDER[EARLY:-1]:
            rs_send[k] = project(k).astype(BF16)
            send_part(k)
        own = project(0)

    with jax.named_scope("query_send"):
        qs = {}
        for k in ORDER[:-1]:
            part = other_k if k % 2 else mine_k
            qs[k] = remote(queries.at[:, part], q_v.at[k], q_ss.at[k], q_rs.at[k], tc_peer(0, k))
            qs[k].start()
        load_q.wait()
        qc = {0: remote(q_v.at[0], q_v.at[8], qc_ss.at[0], qc_rs.at[0], tc_peer(1, 0))}
        qc[0].start()

    with jax.named_scope("grad_part"):
        load_wo.wait()
        load_g.wait()
        pout = dot_nt(wo_v[...], g_v[...]).astype(BF16)
        pout = jnp.concatenate([pout[:, :SEQ], pout[:, SEQ:]], axis=0)

    with jax.named_scope("places"):
        row = lax.broadcasted_iota(jnp.int32, (512, LANES), 0)
        lane = lax.broadcasted_iota(jnp.int32, (512, LANES), 1)
        b_, k_ = row // 256, (row // 64) % 4
        x_, z_, s_ = (row // 16) % 4, (row // 2) % 8, row % 2
        y_hi, y_lo = ((y // 2) + k_ // 2) % 2, (y + k_) % 2
        src_c = (c + b_) % 2
        src_t = (y_hi * 2 + y_lo) * 2 + x_ % 2
        target = (((x_ // 2) * 8 + z_) * 2 + src_c) * 16 + src_t * 2 + s_
        for block in range(4):
            perm[:, block * LANES : (block + 1) * LANES] = jnp.where(
                target == lane + block * LANES, 1.0, 0.0
            ).astype(BF16)

    with jax.named_scope("part_wait"):
        total = own
        for k in ORDER[:-1]:
            rs[k].wait_recv()
            total = total + rs_recv[k].astype(F32)
    with jax.named_scope("outer"):
        pin = total.T
        hi = pin.astype(BF16)
        lo = (pin - hi.astype(F32)).astype(BF16)
        r_v[...] = (dot_nt(hi, pout) + dot_nt(lo, pout)) * (SEQ ** -0.5)
        left = lax.broadcasted_iota(jnp.int32, (RANK // 2, LANES), 1) < RANK
        even, odd = r_v[pl.ds(0, 32, stride=2), :], r_v[pl.ds(1, 32, stride=2), :]
        f0 = jnp.where(left, even, pltpu.roll(odd, RANK, 1)).astype(BF16)
        even, odd = r_v[pl.ds(RANK, 32, stride=2), :], r_v[pl.ds(RANK + 1, 32, stride=2), :]
        f1 = jnp.where(left, pltpu.roll(even, RANK, 1), odd).astype(BF16)
        for half in range(2):
            cut = slice(half * TILES, (half + 1) * TILES)
            f_send[half, :TILES] = f0[cut]
            f_send[half, TILES:] = f1[cut]

    with jax.named_scope("feature_send"):
        fs = {}
        for n, (dx, dz) in reversed(list(enumerate(xz_all))):
            px, pz = ahead(dx, dz)
            src = f_send.at[lax.rem(xl + dx, 2)]
            fs[n] = remote(src, f_recv.at[n], f_ss.at[n], f_rs.at[n], at(px, pz))
            fs[n].start()

    with jax.named_scope("query_core"):
        for k in ORDER[:-1][::-1]:
            qs[k].wait_recv()
            qc[k] = remote(q_v.at[k], q_v.at[8 + k], qc_ss.at[k], qc_rs.at[k], tc_peer(1, 0))
            qc[k].start()

    def spread(px, pz, block):
        both = block.astype(F32)
        for s in range(2):
            first = (px * 8 + pz) * 2 + s
            feats[pl.ds(first, TILES, stride=PITCH), :] = both[s * TILES : (s + 1) * TILES]

    with jax.named_scope("feature_wait"):
        spread(x, z, f_send[xl])
        for n, (dx, dz) in enumerate(xz_all):
            fs[n].wait_recv()
            spread(*behind(dx, dz), f_recv[n])
    with jax.named_scope("query_wait"):
        for k in range(8):
            qc[k].wait_recv()

    with jax.named_scope("score_dot"):
        right = jnp.concatenate(
            [feats[i * PITCH : i * PITCH + 64, :].astype(BF16) for i in range(TILES)], axis=1
        )
        scores = dot_nt(q_v[...].reshape(256, HALF_K), right) * (1.0 / RANK)
        scores = scores.reshape(16, 2, 8, 64)
        s_send[...] = jnp.concatenate([scores[:, 0], scores[:, 1]], axis=2)

    with jax.named_scope("score_send"):
        ssd = {}
        for b, k in [(b, k) for k in ORDER for b in (1, 0) if b or k]:
            slot = b * 8 + k
            ssd[slot] = remote(
                s_send.at[slot], s_recv.at[slot], s_ss.at[slot], s_rs.at[slot], tc_peer(b, k)
            )
            ssd[slot].start()
    with jax.named_scope("score_wait"):
        for slot in ssd:
            ssd[slot].wait_recv()
    with jax.named_scope("place"):
        left = lax.broadcasted_iota(jnp.int32, (8, LANES), 1) < 64
        upper, lower = [], []
        for g in range(4):
            pair = []
            for j in range(2):
                slot = g * 4 + j * 2
                first = s_recv[slot] if slot else s_send[0]
                pair.append(first + s_recv[slot + 1])
            upper.append(jnp.where(left, pair[0], pltpu.roll(pair[1], 64, 1)))
            lower.append(jnp.where(left, pltpu.roll(pair[0], 64, 1), pair[1]))
        wide = jnp.concatenate(
            [jnp.concatenate(upper, axis=1), jnp.concatenate(lower, axis=1)], axis=0
        )
        p1 = wide.astype(BF16)
        rest = wide - p1.astype(F32)
        p2 = rest.astype(BF16)
        p3 = (rest - p2.astype(F32)).astype(BF16)
        placed = dot_nn(jnp.concatenate([p1, p2, p3], axis=0), perm[...])
        out[...] = (placed[:16] + placed[16:32]) + placed[32:]

    with jax.named_scope("send_wait"):
        for sends in (rs, qs, qc, fs, ssd):
            for copy in sends.values():
                copy.wait_send()


def body(hidden, grad_out, proj_in, proj_out, queries):
    dma = pltpu.SemaphoreType.DMA
    scratch = [
        pltpu.VMEM((8, 256, FF_PART), BF16),
        pltpu.VMEM((256, D), BF16),
        pltpu.VMEM((2, LANES, FF_PART), BF16),
        pltpu.VMEM((RANK, D), BF16),
        pltpu.VMEM((16, 16, HALF_K), BF16),
        pltpu.VMEM((8, SEQ, LANES), BF16),
        pltpu.VMEM((8, SEQ, LANES), BF16),
        pltpu.VMEM((LANES, LANES), F32),
        pltpu.VMEM((2, 2 * TILES, LANES), BF16),
        pltpu.VMEM((31, 2 * TILES, LANES), BF16),
        pltpu.VMEM((TILES * PITCH, LANES), F32),
        pltpu.VMEM((16, 8, LANES), F32),
        pltpu.VMEM((16, 8, LANES), F32),
        pltpu.VMEM((512, 512), BF16),
        dma((8,)), dma((5,)), dma((8,)), dma((8,)), dma((8,)), dma((8,)),
        dma((8,)), dma((8,)), dma((31,)), dma((31,)), dma((16,)), dma((16,)),
    ]
    return pl.pallas_call(
        kernel,
        out_shape=jax.ShapeDtypeStruct((16, 512), F32),
        in_specs=[pl.BlockSpec(memory_space=pltpu.HBM)] * 5,
        out_specs=pl.BlockSpec(memory_space=pltpu.VMEM),
        scratch_shapes=scratch,
        compiler_params=pltpu.CompilerParams(
            collective_id=0, has_side_effects=True, vmem_limit_bytes=56418304
        ),
    )(hidden, grad_out, proj_in, proj_out, queries)


def solution(mesh):
    placed = (
        P("dp", "tensor"),
        P(("dp", "tensor"), None),
        P(None, "tensor"),
        P(),
        P(("dp", "tensor"), None),
    )
    return jax.shard_map(
        body, mesh=mesh, in_specs=placed, out_specs=P(("dp", "tensor"), None), check_vma=False
    )
```

```python
import jax
import jax.numpy as jnp
from jax import lax
from jax.experimental import pallas as pl
from jax.experimental.pallas import tpu as pltpu
from jax.sharding import PartitionSpec as P

MESH = pl.DeviceIdType.MESH
BF16, F32 = jnp.bfloat16, jnp.float32
SEQ = 128
RANK = 64
LANES = 128
FF_PART = 1792
D = 4096
HALF_K = RANK * RANK // 2
TILES = HALF_K // LANES
PITCH = 72

ORDER = (5, 4, 3, 7, 2, 6, 1, 0)
STEPS = ((0, ORDER[:4]), (0, ORDER[4:]), (1, ORDER[:4]), (1, ORDER[4:]))
SLOTS = ((0, 0), (0, 1), (1, 0), (3, 0), (1, 1), (3, 1), (2, 0), (2, 1))


def flip(value, mask, bits):
    result = 0
    for bit in range(bits):
        digit = lax.rem(lax.div(value, 1 << bit), 2)
        result = result + (1 << bit) * (1 - digit if (mask >> bit) & 1 else digit)
    return result


def dot_nt(a, b):
    return lax.dot_general(a, b, (((1,), (1,)), ((), ())), preferred_element_type=F32)


def dot_nn(a, b):
    return lax.dot_general(a, b, (((1,), (0,)), ((), ())), preferred_element_type=F32)


def kernel(
    hidden, grad_out, proj_in, proj_out, queries, out,
    x_v, g_v, wi_v, wo_v, q_v, q_o, rs_send, rs_recv, r_v, f_send, f_recv, feats, s_send, s_recv, perm,
    x_sem, w_sem, rs_ss, rs_rs, q_ss, q_rs, qc_ss, qc_rs, f_ss, f_rs, s_ss, s_rs, wave,
):
    dp, t = lax.axis_index("dp"), lax.axis_index("tensor")
    c, z, xh = lax.rem(dp, 2), lax.rem(lax.div(dp, 2), 8), lax.div(dp, 16)
    y, xl = lax.div(t, 2), lax.rem(t, 2)
    x = xh * 2 + xl

    def t_peer(k):
        return (dp, flip(t, k, 3))

    def tc_peer(b, dy, kx):
        return (dp + 1 - 2 * c if b else dp, lax.rem(y + dy, 4) * 2 + (1 - xl if kx else xl))

    def at(px, pz):
        return ((lax.div(px, 2) * 8 + pz) * 2 + c, y * 2 + lax.rem(px, 2))

    def ahead(dx, dz):
        return lax.rem(x + dx, 4), lax.rem(z + dz, 8)

    def behind(dx, dz):
        return lax.rem(x + 4 - dx, 4), lax.rem(z + 8 - dz, 8)

    tc_all = [(b, *o) for b in (0, 1) for o in SLOTS if b or o != (0, 0)]
    tc_all.sort(key=lambda o: -2 * (min(o[1], 4 - o[1]) + o[2]) - o[0])
    xz_all = [(dx, dz) for dx in range(4) for dz in range(8) if dx or dz]
    xz_all.sort(key=lambda o: -min(o[0], 4 - o[0]) - min(o[1], 8 - o[1]))

    def remote(src, dst, ss, rs, peer):
        return pltpu.make_async_remote_copy(
            src_ref=src, dst_ref=dst, send_sem=ss, recv_sem=rs, device_id=peer, device_id_type=MESH
        )

    def settle(ref, sem):
        pltpu.make_async_copy(ref, ref, sem).wait()

    def tell(sem, peer):
        pl.semaphore_signal(sem, inc=1, device_id=peer, device_id_type=MESH)

    mine_k = pl.ds(pl.multiple_of(xl * HALF_K, HALF_K), HALF_K)
    other_k = pl.ds(pl.multiple_of((1 - xl) * HALF_K, HALF_K), HALF_K)
    load_wi = pltpu.make_async_copy(proj_in, wi_v, w_sem.at[0])
    load_wo = pltpu.make_async_copy(proj_out, wo_v, w_sem.at[1])
    load_g = pltpu.make_async_copy(grad_out, g_v, w_sem.at[2])
    load_q = pltpu.make_async_copy(queries.at[:, mine_k], q_v.at[0], w_sem.at[3])
    load_o = pltpu.make_async_copy(queries.at[:, other_k], q_o, w_sem.at[4])

    def load_step(step):
        s, ks = STEPS[step]
        for n, k in enumerate(ks):
            rows = pl.ds(pl.multiple_of(flip(t, k, 3) * 256 + s * SEQ, SEQ), SEQ)
            pltpu.make_async_copy(hidden.at[rows], x_v.at[step, n], x_sem.at[step]).start()

    load_q.start()
    load_o.start()
    load_wi.start()
    load_step(0)

    with jax.named_scope("greet"):
        barrier = pltpu.get_barrier_semaphore()
        greeted = [tc_peer(0, *o) for o in SLOTS[:0:-1]]
        greeted += [at(*ahead(0, dz)) for dz in (2, 6, 1, 7)] + [at(*ahead(2, 0))]
        greeted += [at(lax.rem(x + 3 + 2 * xl, 4), z), tc_peer(1, 0, 0)]
        for peer in greeted:
            tell(barrier, peer)

    for step in range(1, 4):
        load_step(step)
    load_wo.start()
    load_g.start()

    with jax.named_scope("entry_wait"):
        pl.semaphore_wait(barrier, len(greeted))

    with jax.named_scope("heard_0"):
        for dz in (2, 6, 1, 7):
            tell(wave.at[1], at(*ahead(0, dz)))
        tell(wave.at[0], tc_peer(1, 0, 0))

    with jax.named_scope("query_send"):
        load_q.wait()
        load_o.wait()
        remote(q_v.at[0], q_v.at[8], qc_ss, qc_rs, tc_peer(1, 0, 0)).start()
        remote(q_o, q_v.at[1], q_ss, q_rs.at[0], tc_peer(0, 0, 1)).start()
        remote(q_v.at[0], q_v.at[3], q_ss, q_rs.at[1], tc_peer(0, 1, 0)).start()
        remote(q_v.at[0], q_v.at[2], q_ss, q_rs.at[1], tc_peer(0, 3, 0)).start()

    own = {}

    def project(step):
        s, ks = STEPS[step]
        settle(x_v.at[step], x_sem.at[step])
        parts = dot_nt(wi_v[...], x_v[step].reshape(4 * SEQ, FF_PART))
        for n, k in enumerate(ks):
            part = parts[:, n * SEQ : (n + 1) * SEQ]
            if k:
                rs_send[s, k] = part.astype(BF16)
            else:
                own[s] = part

    def send_parts(step):
        s, ks = STEPS[step]
        for k in ks:
            if k:
                remote(rs_send.at[s, k], rs_recv.at[s, k], rs_ss, rs_rs.at[s], t_peer(k)).start()

    load_wi.wait()
    with jax.named_scope("hidden_0"):
        project(0)
        send_parts(0)
    with jax.named_scope("hidden_1"):
        project(1)
        send_parts(1)
    with jax.named_scope("hidden_2"):
        project(2)
        send_parts(2)
    with jax.named_scope("hidden_3"):
        project(3)
        send_parts(3)

    with jax.named_scope("heard_1"):
        pl.semaphore_wait(wave.at[1], 4)
        for dz in (4, 3, 5):
            tell(wave.at[2], at(*ahead(0, dz)))
    with jax.named_scope("query_2"):
        settle(q_v.at[1], q_rs.at[0])
        remote(q_v.at[1], q_v.at[5], q_ss, q_rs.at[2], tc_peer(0, 1, 0)).start()
        remote(q_v.at[1], q_v.at[4], q_ss, q_rs.at[2], tc_peer(0, 3, 0)).start()
    with jax.named_scope("grad_part"):
        load_wo.wait()
        load_g.wait()
        pout = dot_nt(wo_v[...], g_v[...]).astype(BF16)

    with jax.named_scope("heard_2"):
        pl.semaphore_wait(wave.at[0], 1)
        pl.semaphore_wait(wave.at[2], 3)

    def features(s):
        with jax.named_scope("part_wait_%d" % s):
            settle(rs_recv.at[s, pl.ds(1, 7)], rs_rs.at[s])
        with jax.named_scope("outer"):
            pin = own[s]
            for k in range(1, 8):
                pin = pin + rs_recv[s, k].astype(F32)
            hi = pin.astype(BF16)
            lo = (pin - hi.astype(F32)).astype(BF16)
            right = pout[:, s * SEQ : (s + 1) * SEQ]
            twice = jnp.concatenate([right, right], axis=0)
            r_v[...] = (dot_nt(hi, twice) + dot_nt(lo, twice)) * (SEQ ** -0.5)
            left = lax.broadcasted_iota(jnp.int32, (RANK // 2, LANES), 1) < RANK
            even, odd = r_v[pl.ds(0, 32, stride=2), :], r_v[pl.ds(1, 32, stride=2), :]
            f = jnp.where(left, even, odd).astype(BF16)
            f_send[s, 0] = f[:TILES]
            f_send[s, 1] = f[TILES:]
        with jax.named_scope("feature_send_%d" % s):
            for n, (dx, dz) in enumerate(xz_all):
                src = f_send.at[s, lax.rem(xl + dx, 2)]
                remote(src, f_recv.at[s, n], f_ss, f_rs, at(*ahead(dx, dz))).start()

    features(0)
    features(1)
    with jax.named_scope("query_3"):
        first, last = pl.ds(0, HALF_K // 2), pl.ds(HALF_K // 2, HALF_K // 2)
        for kx in range(2):
            settle(q_v.at[pl.ds(2 + 2 * kx, 2)], q_rs.at[1 + kx])
            for slot, part, dy in ((3, first, 1), (2, last, 3)):
                remote(
                    q_v.at[slot + 2 * kx, :, part], q_v.at[6 + kx, :, part], q_ss, q_rs.at[3],
                    tc_peer(0, dy, 0),
                ).start()
        remote(q_v.at[pl.ds(1, 5)], q_v.at[pl.ds(9, 5)], qc_ss, qc_rs, tc_peer(1, 0, 0)).start()

    with jax.named_scope("places"):
        row = lax.broadcasted_iota(jnp.int32, (512, LANES), 0)
        lane = lax.broadcasted_iota(jnp.int32, (512, LANES), 1)
        b_, dy_ = row // 256, (row // 64) % 4
        x_, z_, s_ = (row // 16) % 4, (row // 2) % 8, row % 2
        src_c = (c + b_) % 2
        src_t = ((y + dy_) % 4) * 2 + x_ % 2
        target = (((x_ // 2) * 8 + z_) * 2 + src_c) * 16 + src_t * 2 + s_
        for block in range(4):
            perm[:, block * LANES : (block + 1) * LANES] = jnp.where(
                target == lane + block * LANES, 1.0, 0.0
            ).astype(BF16)

    with jax.named_scope("query_core"):
        settle(q_v.at[pl.ds(6, 2)], q_rs.at[3])
        remote(q_v.at[pl.ds(6, 2)], q_v.at[pl.ds(14, 2)], qc_ss, qc_rs, tc_peer(1, 0, 0)).start()

    def spread(px, pz, s, block):
        feats[pl.ds((px * 8 + pz) * 2 + s, TILES, stride=PITCH), :] = block.astype(F32)

    with jax.named_scope("feature_wait"):
        settle(f_recv, f_rs)
    with jax.named_scope("spread"):
        for s in range(2):
            spread(x, z, s, f_send[s, xl])
            for n, (dx, dz) in enumerate(xz_all):
                spread(*behind(dx, dz), s, f_recv[s, n])
    with jax.named_scope("query_wait"):
        settle(q_v.at[pl.ds(8, 8)], qc_rs)

    with jax.named_scope("score_dot"):
        right = jnp.concatenate(
            [feats[i * PITCH : i * PITCH + 64, :].astype(BF16) for i in range(TILES)], axis=1
        )
        scores = dot_nt(q_v[...].reshape(256, HALF_K), right) * (1.0 / RANK)
        scores = scores.reshape(16, 2, 8, 64)
        s_send[...] = jnp.concatenate([scores[:, 0], scores[:, 1]], axis=2)

    with jax.named_scope("score_send"):
        for b, dy, kx in tc_all:
            slot = b * 8 + SLOTS.index((dy, kx))
            there = b * 8 + SLOTS.index(((4 - dy) % 4, kx))
            remote(s_send.at[slot], s_recv.at[there], s_ss, s_rs, tc_peer(b, dy, kx)).start()
    with jax.named_scope("score_wait"):
        settle(s_recv.at[pl.ds(1, 15)], s_rs)
    with jax.named_scope("place"):
        left = lax.broadcasted_iota(jnp.int32, (8, LANES), 1) < 64
        upper, lower = [], []
        for g in range(4):
            pair = []
            for dy in range(2 * (g % 2), 2 * (g % 2) + 2):
                one, two = [(g // 2) * 8 + SLOTS.index((dy, kx)) for kx in range(2)]
                pair.append((s_recv[one] if one else s_send[0]) + s_recv[two])
            upper.append(jnp.where(left, pair[0], pltpu.roll(pair[1], 64, 1)))
            lower.append(jnp.where(left, pltpu.roll(pair[0], 64, 1), pair[1]))
        wide = jnp.concatenate(
            [jnp.concatenate(upper, axis=1), jnp.concatenate(lower, axis=1)], axis=0
        )
        p1 = wide.astype(BF16)
        rest = wide - p1.astype(F32)
        p2 = rest.astype(BF16)
        p3 = (rest - p2.astype(F32)).astype(BF16)
        placed = dot_nn(jnp.concatenate([p1, p2, p3], axis=0), perm[...])
        out[...] = (placed[:16] + placed[16:32]) + placed[32:]

    with jax.named_scope("send_wait"):
        settle(rs_send.at[:, pl.ds(1, 7)], rs_ss)
        settle(q_v.at[pl.ds(0, 7)], q_ss)
        settle(q_v.at[pl.ds(0, 8)], qc_ss)
        settle(f_recv, f_ss)
        settle(s_send.at[pl.ds(1, 15)], s_ss)


def body(hidden, grad_out, proj_in, proj_out, queries):
    dma = pltpu.SemaphoreType.DMA
    scratch = [
        pltpu.VMEM((4, 4, SEQ, FF_PART), BF16),
        pltpu.VMEM((256, D), BF16),
        pltpu.VMEM((RANK, FF_PART), BF16),
        pltpu.VMEM((RANK, D), BF16),
        pltpu.VMEM((16, 16, HALF_K), BF16),
        pltpu.VMEM((16, HALF_K), BF16),
        pltpu.VMEM((2, 8, RANK, SEQ), BF16),
        pltpu.VMEM((2, 8, RANK, SEQ), BF16),
        pltpu.VMEM((RANK, LANES), F32),
        pltpu.VMEM((2, 2, TILES, LANES), BF16),
        pltpu.VMEM((2, 31, TILES, LANES), BF16),
        pltpu.VMEM((TILES * PITCH, LANES), F32),
        pltpu.VMEM((16, 8, LANES), F32),
        pltpu.VMEM((16, 8, LANES), F32),
        pltpu.VMEM((512, 512), BF16),
        dma((4,)), dma((5,)), dma, dma((2,)), dma, dma((4,)), *[dma] * 6,
        pltpu.SemaphoreType.REGULAR((3,)),
    ]
    return pl.pallas_call(
        kernel,
        out_shape=jax.ShapeDtypeStruct((16, 512), F32),
        in_specs=[pl.BlockSpec(memory_space=pltpu.HBM)] * 5,
        out_specs=pl.BlockSpec(memory_space=pltpu.VMEM),
        scratch_shapes=scratch,
        compiler_params=pltpu.CompilerParams(
            collective_id=0, has_side_effects=True, vmem_limit_bytes=56418304
        ),
    )(hidden, grad_out, proj_in, proj_out, queries)


def solution(mesh):
    placed = (
        P("dp", "tensor"),
        P(("dp", "tensor"), None),
        P(None, "tensor"),
        P(),
        P(("dp", "tensor"), None),
    )
    return jax.shard_map(
        body, mesh=mesh, in_specs=placed, out_specs=P(("dp", "tensor"), None), check_vma=False
    )
```

```python
import jax
import jax.numpy as jnp
from jax import lax
from jax.experimental import pallas as pl
from jax.experimental.pallas import tpu as pltpu
from jax.sharding import PartitionSpec as P

MESH = pl.DeviceIdType.MESH
BF16, F32 = jnp.bfloat16, jnp.float32
SEQ = 128
RANK = 64
LANES = 128
FF_PART = 1792
D = 4096
HALF_K = RANK * RANK // 2
TILES = HALF_K // LANES
PITCH = 72

ORDER = (5, 4, 3, 7, 2, 6, 1, 0)
STEPS = ((0, ORDER[:4]), (0, ORDER[4:]), (1, ORDER[:3]), (1, ORDER[3:6]), (1, ORDER[6:]))
FIRST = (0, 4, 8, 11, 14)
SLOTS = ((0, 0), (0, 1), (1, 0), (3, 0), (1, 1), (3, 1), (2, 0), (2, 1))


def flip(value, mask, bits):
    result = 0
    for bit in range(bits):
        digit = lax.rem(lax.div(value, 1 << bit), 2)
        result = result + (1 << bit) * (1 - digit if (mask >> bit) & 1 else digit)
    return result


def dot_nt(a, b):
    return lax.dot_general(a, b, (((1,), (1,)), ((), ())), preferred_element_type=F32)


def dot_nn(a, b):
    return lax.dot_general(a, b, (((1,), (0,)), ((), ())), preferred_element_type=F32)


def kernel(
    hidden, grad_out, proj_in, proj_out, queries, out,
    x_v, g_v, wi_v, wo_v, q_v, q_o, rs_send, rs_recv, r_v, f_send, f_recv, feats, s_send, s_recv, perm,
    x_sem, w_sem, rs_ss, rs_rs, q_ss, q_rs, qc_ss, qc_rs, f_ss, f_rs, s_ss, s_rs, wave,
):
    dp, t = lax.axis_index("dp"), lax.axis_index("tensor")
    c, z, xh = lax.rem(dp, 2), lax.rem(lax.div(dp, 2), 8), lax.div(dp, 16)
    y, xl = lax.div(t, 2), lax.rem(t, 2)
    x = xh * 2 + xl

    def t_peer(k):
        return (dp, flip(t, k, 3))

    def tc_peer(b, dy, kx):
        return (dp + 1 - 2 * c if b else dp, lax.rem(y + dy, 4) * 2 + (1 - xl if kx else xl))

    def at(px, pz):
        return ((lax.div(px, 2) * 8 + pz) * 2 + c, y * 2 + lax.rem(px, 2))

    def ahead(dx, dz):
        return lax.rem(x + dx, 4), lax.rem(z + dz, 8)

    def behind(dx, dz):
        return lax.rem(x + 4 - dx, 4), lax.rem(z + 8 - dz, 8)

    tc_all = [(b, *o) for b in (0, 1) for o in SLOTS if b or o != (0, 0)]
    tc_all.sort(key=lambda o: -2 * (min(o[1], 4 - o[1]) + o[2]) - o[0])
    xz_all = [(dx, dz) for dx in range(4) for dz in range(8) if dx or dz]
    xz_all.sort(key=lambda o: -min(o[0], 4 - o[0]) - min(o[1], 8 - o[1]))

    def remote(src, dst, ss, rs, peer):
        return pltpu.make_async_remote_copy(
            src_ref=src, dst_ref=dst, send_sem=ss, recv_sem=rs, device_id=peer, device_id_type=MESH
        )

    def settle(ref, sem):
        pltpu.make_async_copy(ref, ref, sem).wait()

    def tell(sem, peer):
        pl.semaphore_signal(sem, inc=1, device_id=peer, device_id_type=MESH)

    mine_k = pl.ds(pl.multiple_of(xl * HALF_K, HALF_K), HALF_K)
    other_k = pl.ds(pl.multiple_of((1 - xl) * HALF_K, HALF_K), HALF_K)
    load_wi = pltpu.make_async_copy(proj_in, wi_v, w_sem.at[0])
    load_wo = pltpu.make_async_copy(proj_out, wo_v, w_sem.at[1])
    load_g = pltpu.make_async_copy(grad_out, g_v, w_sem.at[2])
    load_q = pltpu.make_async_copy(queries.at[:, mine_k], q_v.at[0], w_sem.at[3])
    load_o = pltpu.make_async_copy(queries.at[:, other_k], q_o, w_sem.at[4])

    def load_step(step):
        s, ks = STEPS[step]
        for n, k in enumerate(ks):
            rows = pl.ds(pl.multiple_of(flip(t, k, 3) * 256 + s * SEQ, SEQ), SEQ)
            pltpu.make_async_copy(hidden.at[rows], x_v.at[FIRST[step] + n], x_sem.at[step]).start()

    load_q.start()
    load_o.start()
    load_wi.start()
    load_step(0)

    with jax.named_scope("greet"):
        barrier = pltpu.get_barrier_semaphore()
        greeted = [tc_peer(0, *o) for o in SLOTS[:0:-1]]
        greeted += [at(*ahead(0, dz)) for dz in (2, 6, 1, 7)] + [at(*ahead(2, 0))]
        greeted += [at(lax.rem(x + 3 + 2 * xl, 4), z), tc_peer(1, 0, 0)]
        for peer in greeted:
            tell(barrier, peer)

    for step in range(1, len(STEPS)):
        load_step(step)
    load_wo.start()
    load_g.start()

    with jax.named_scope("entry_wait"):
        pl.semaphore_wait(barrier, len(greeted))

    with jax.named_scope("heard_0"):
        for dz in (2, 6, 1, 7):
            tell(wave.at[1], at(*ahead(0, dz)))
        tell(wave.at[0], tc_peer(1, 0, 0))

    with jax.named_scope("query_send"):
        load_q.wait()
        load_o.wait()
        remote(q_v.at[0], q_v.at[8], qc_ss, qc_rs, tc_peer(1, 0, 0)).start()
        remote(q_o, q_v.at[1], q_ss, q_rs.at[0], tc_peer(0, 0, 1)).start()
        remote(q_v.at[0], q_v.at[3], q_ss, q_rs.at[1], tc_peer(0, 1, 0)).start()
        remote(q_v.at[0], q_v.at[2], q_ss, q_rs.at[1], tc_peer(0, 3, 0)).start()

    own = {}

    def project(step):
        s, ks = STEPS[step]
        rows = pl.ds(FIRST[step], len(ks))
        settle(x_v.at[rows], x_sem.at[step])
        parts = dot_nt(wi_v[...], x_v[rows].reshape(len(ks) * SEQ, FF_PART))
        for n, k in enumerate(ks):
            part = parts[:, n * SEQ : (n + 1) * SEQ]
            if k:
                rs_send[s, k] = part.astype(BF16)
            else:
                own[s] = part

    def send_parts(step):
        s, ks = STEPS[step]
        for k in ks:
            if k:
                remote(rs_send.at[s, k], rs_recv.at[s, k], rs_ss, rs_rs.at[s], t_peer(k)).start()

    load_wi.wait()
    with jax.named_scope("hidden_0"):
        project(0)
        send_parts(0)
    with jax.named_scope("hidden_1"):
        project(1)
        send_parts(1)
    with jax.named_scope("hidden_2"):
        project(2)
        send_parts(2)
    with jax.named_scope("heard_1"):
        pl.semaphore_wait(wave.at[1], 4)
        for dz in (4, 3, 5):
            tell(wave.at[2], at(*ahead(0, dz)))
    with jax.named_scope("hidden_3"):
        project(3)
        send_parts(3)
    with jax.named_scope("hidden_4"):
        project(4)
        send_parts(4)

    with jax.named_scope("grad_part"):
        load_wo.wait()
        load_g.wait()
        pout = dot_nt(wo_v[...], g_v[...]).astype(BF16)

    with jax.named_scope("heard_2"):
        pl.semaphore_wait(wave.at[0], 1)
        pl.semaphore_wait(wave.at[2], 3)

    def features(s):
        with jax.named_scope("part_wait_%d" % s):
            settle(rs_recv.at[s, pl.ds(1, 7)], rs_rs.at[s])
        with jax.named_scope("outer"):
            pin = own[s]
            for k in range(1, 8):
                pin = pin + rs_recv[s, k].astype(F32)
            hi = pin.astype(BF16)
            lo = (pin - hi.astype(F32)).astype(BF16)
            right = pout[:, s * SEQ : (s + 1) * SEQ]
            twice = jnp.concatenate([right, right], axis=0)
            r_v[:RANK] = (dot_nt(hi, twice) + dot_nt(lo, twice)) * (SEQ ** -0.5)
            left = lax.broadcasted_iota(jnp.int32, (RANK // 2, LANES), 1) < RANK
            even, odd = r_v[pl.ds(0, 32, stride=2), :], r_v[pl.ds(1, 32, stride=2), :]
            f = jnp.where(left, even, odd).astype(BF16)
            f_send[s, 0] = f[:TILES]
            f_send[s, 1] = f[TILES:]
        with jax.named_scope("feature_send_%d" % s):
            for n, (dx, dz) in enumerate(xz_all):
                src = f_send.at[s, lax.rem(xl + dx, 2)]
                remote(src, f_recv.at[s, n], f_ss, f_rs, at(*ahead(dx, dz))).start()

    with jax.named_scope("query_2"):
        settle(q_v.at[1], q_rs.at[0])
        remote(q_v.at[1], q_v.at[5], q_ss, q_rs.at[2], tc_peer(0, 1, 0)).start()
        remote(q_v.at[1], q_v.at[4], q_ss, q_rs.at[2], tc_peer(0, 3, 0)).start()
    features(0)
    features(1)
    with jax.named_scope("query_3"):
        first, last = pl.ds(0, HALF_K // 2), pl.ds(HALF_K // 2, HALF_K // 2)
        for kx in range(2):
            settle(q_v.at[pl.ds(2 + 2 * kx, 2)], q_rs.at[1 + kx])
            for slot, part, dy in ((3, first, 1), (2, last, 3)):
                remote(
                    q_v.at[slot + 2 * kx, :, part], q_v.at[6 + kx, :, part], q_ss, q_rs.at[3],
                    tc_peer(0, dy, 0),
                ).start()
        remote(q_v.at[pl.ds(1, 5)], q_v.at[pl.ds(9, 5)], qc_ss, qc_rs, tc_peer(1, 0, 0)).start()

    with jax.named_scope("places"):
        row = lax.broadcasted_iota(jnp.int32, (512, LANES), 0)
        lane = lax.broadcasted_iota(jnp.int32, (512, LANES), 1)
        b_, dy_ = row // 256, (row // 64) % 4
        x_, z_, s_ = (row // 16) % 4, (row // 2) % 8, row % 2
        src_c = (c + b_) % 2
        src_t = ((y + dy_) % 4) * 2 + x_ % 2
        target = (((x_ // 2) * 8 + z_) * 2 + src_c) * 16 + src_t * 2 + s_
        for block in range(4):
            perm[:, block * LANES : (block + 1) * LANES] = jnp.where(
                target == lane + block * LANES, 1.0, 0.0
            ).astype(BF16)

    with jax.named_scope("query_core"):
        settle(q_v.at[pl.ds(6, 2)], q_rs.at[3])
        remote(q_v.at[pl.ds(6, 2)], q_v.at[pl.ds(14, 2)], qc_ss, qc_rs, tc_peer(1, 0, 0)).start()

    def spread(px, pz, s, block):
        feats[pl.ds((px * 8 + pz) * 2 + s, TILES, stride=PITCH), :] = block.astype(F32)

    with jax.named_scope("feature_wait"):
        settle(f_recv, f_rs)
    with jax.named_scope("spread"):
        for s in range(2):
            spread(x, z, s, f_send[s, xl])
            for n, (dx, dz) in enumerate(xz_all):
                spread(*behind(dx, dz), s, f_recv[s, n])
    with jax.named_scope("query_wait"):
        settle(q_v.at[pl.ds(8, 8)], qc_rs)

    with jax.named_scope("score_dot"):
        right = jnp.concatenate(
            [feats[i * PITCH : i * PITCH + 64, :].astype(BF16) for i in range(TILES)], axis=1
        )
        scores = dot_nt(q_v[...].reshape(256, HALF_K), right) * (1.0 / RANK)
        scores = scores.reshape(16, 2, 8, 64)
        s_send[...] = jnp.concatenate([scores[:, 0], scores[:, 1]], axis=2)

    with jax.named_scope("score_send"):
        for b, dy, kx in tc_all:
            slot = b * 8 + SLOTS.index((dy, kx))
            there = b * 8 + SLOTS.index(((4 - dy) % 4, kx))
            remote(s_send.at[slot], s_recv.at[there], s_ss, s_rs, tc_peer(b, dy, kx)).start()
    with jax.named_scope("score_wait"):
        settle(s_recv.at[pl.ds(1, 15)], s_rs)
    with jax.named_scope("place"):
        left = lax.broadcasted_iota(jnp.int32, (8, LANES), 1) < 64
        upper, lower = [], []
        for g in range(4):
            pair = []
            for dy in range(2 * (g % 2), 2 * (g % 2) + 2):
                one, two = [(g // 2) * 8 + SLOTS.index((dy, kx)) for kx in range(2)]
                pair.append((s_recv[one] if one else s_send[0]) + s_recv[two])
            upper.append(jnp.where(left, pair[0], pltpu.roll(pair[1], 64, 1)))
            lower.append(jnp.where(left, pltpu.roll(pair[0], 64, 1), pair[1]))
        wide = jnp.concatenate(
            [jnp.concatenate(upper, axis=1), jnp.concatenate(lower, axis=1)], axis=0
        )
        p1 = wide.astype(BF16)
        rest = wide - p1.astype(F32)
        p2 = rest.astype(BF16)
        p3 = (rest - p2.astype(F32)).astype(BF16)
        placed = dot_nn(jnp.concatenate([p1, p2, p3], axis=0), perm[...])
        out[...] = (placed[:16] + placed[16:32]) + placed[32:]

    with jax.named_scope("send_wait"):
        settle(rs_send.at[:, pl.ds(1, 7)], rs_ss)
        settle(q_v.at[pl.ds(0, 7)], q_ss)
        settle(q_v.at[pl.ds(0, 8)], qc_ss)
        settle(f_recv, f_ss)
        settle(s_send.at[pl.ds(1, 15)], s_ss)


def body(hidden, grad_out, proj_in, proj_out, queries):
    dma = pltpu.SemaphoreType.DMA
    scratch = [
        pltpu.VMEM((16, SEQ, FF_PART), BF16),
        pltpu.VMEM((256, D), BF16),
        pltpu.VMEM((RANK, FF_PART), BF16),
        pltpu.VMEM((RANK, D), BF16),
        pltpu.VMEM((16, 16, HALF_K), BF16),
        pltpu.VMEM((16, HALF_K), BF16),
        pltpu.VMEM((2, 8, RANK, SEQ), BF16),
        pltpu.VMEM((2, 8, RANK, SEQ), BF16),
        pltpu.VMEM((RANK + 8, LANES), F32),
        pltpu.VMEM((2, 2, TILES, LANES), BF16),
        pltpu.VMEM((2, 31, TILES, LANES), BF16),
        pltpu.VMEM(((TILES + 1) * PITCH, LANES), F32),
        pltpu.VMEM((16, 8, LANES), F32),
        pltpu.VMEM((16, 8, LANES), F32),
        pltpu.VMEM((512, 512), BF16),
        dma((5,)), dma((5,)), dma, dma((2,)), dma, dma((4,)), *[dma] * 6,
        pltpu.SemaphoreType.REGULAR((3,)),
    ]
    return pl.pallas_call(
        kernel,
        out_shape=jax.ShapeDtypeStruct((16, 512), F32),
        in_specs=[pl.BlockSpec(memory_space=pltpu.HBM)] * 5,
        out_specs=pl.BlockSpec(memory_space=pltpu.VMEM),
        scratch_shapes=scratch,
        compiler_params=pltpu.CompilerParams(
            collective_id=0, has_side_effects=True, vmem_limit_bytes=56418304
        ),
    )(hidden, grad_out, proj_in, proj_out, queries)


def solution(mesh):
    placed = (
        P("dp", "tensor"),
        P(("dp", "tensor"), None),
        P(None, "tensor"),
        P(),
        P(("dp", "tensor"), None),
    )
    return jax.shard_map(
        body, mesh=mesh, in_specs=placed, out_specs=P(("dp", "tensor"), None), check_vma=False
    )
```

```python
import jax
import jax.numpy as jnp
from jax import lax
from jax.experimental import pallas as pl
from jax.experimental.pallas import tpu as pltpu
from jax.sharding import PartitionSpec as P

MESH = pl.DeviceIdType.MESH
BF16, F32 = jnp.bfloat16, jnp.float32
SEQ = 128
RANK = 64
LANES = 128
FF_PART = 1792
D = 4096
HALF_K = RANK * RANK // 2
TILES = HALF_K // LANES
PITCH = 72

ORDER = (5, 4, 3, 7, 2, 6, 1, 0)
STEPS = ((0, ORDER[:4]), (0, ORDER[4:]), (1, ORDER[:3]), (1, ORDER[3:6]), (1, ORDER[6:]))
FIRST = (0, 4, 8, 11, 14)
SLOTS = ((0, 0), (0, 1), (1, 0), (3, 0), (1, 1), (3, 1), (2, 0), (2, 1))


def flip(value, mask, bits):
    result = 0
    for bit in range(bits):
        digit = lax.rem(lax.div(value, 1 << bit), 2)
        result = result + (1 << bit) * (1 - digit if (mask >> bit) & 1 else digit)
    return result


def dot_nt(a, b):
    return lax.dot_general(a, b, (((1,), (1,)), ((), ())), preferred_element_type=F32)


def dot_nn(a, b):
    return lax.dot_general(a, b, (((1,), (0,)), ((), ())), preferred_element_type=F32)


def kernel(
    hidden, grad_out, proj_in, proj_out, queries, out,
    x_v, g_v, wi_v, wo_v, q_v, q_o, rs_send, rs_recv, r_v, f_send, f_recv, feats, s_send, s_recv, perm,
    x_sem, w_sem, rs_ss, rs_rs, q_ss, q_rs, qc_ss, qc_rs, f_ss, f_rs, s_ss, s_rs, wave,
):
    dp, t = lax.axis_index("dp"), lax.axis_index("tensor")
    c, z, xh = lax.rem(dp, 2), lax.rem(lax.div(dp, 2), 8), lax.div(dp, 16)
    y, xl = lax.div(t, 2), lax.rem(t, 2)
    x = xh * 2 + xl

    def t_peer(k):
        return (dp, flip(t, k, 3))

    def tc_peer(b, dy, kx):
        return (dp + 1 - 2 * c if b else dp, lax.rem(y + dy, 4) * 2 + (1 - xl if kx else xl))

    def at(px, pz):
        return ((lax.div(px, 2) * 8 + pz) * 2 + c, y * 2 + lax.rem(px, 2))

    def ahead(dx, dz):
        return lax.rem(x + dx, 4), lax.rem(z + dz, 8)

    def behind(dx, dz):
        return lax.rem(x + 4 - dx, 4), lax.rem(z + 8 - dz, 8)

    tc_all = [(b, *o) for b in (0, 1) for o in SLOTS if b or o != (0, 0)]
    tc_all.sort(key=lambda o: -2 * (min(o[1], 4 - o[1]) + o[2]) - o[0])
    xz_all = [(dx, dz) for dx in range(4) for dz in range(8) if dx or dz]
    xz_all.sort(key=lambda o: -min(o[0], 4 - o[0]) - min(o[1], 8 - o[1]))

    def remote(src, dst, ss, rs, peer):
        return pltpu.make_async_remote_copy(
            src_ref=src, dst_ref=dst, send_sem=ss, recv_sem=rs, device_id=peer, device_id_type=MESH
        )

    def settle(ref, sem):
        pltpu.make_async_copy(ref, ref, sem).wait()

    def tell(sem, peer):
        pl.semaphore_signal(sem, inc=1, device_id=peer, device_id_type=MESH)

    mine_k = pl.ds(pl.multiple_of(xl * HALF_K, HALF_K), HALF_K)
    other_k = pl.ds(pl.multiple_of((1 - xl) * HALF_K, HALF_K), HALF_K)
    load_wi = pltpu.make_async_copy(proj_in, wi_v, w_sem.at[0])
    load_wo = pltpu.make_async_copy(proj_out, wo_v, w_sem.at[1])
    load_g = pltpu.make_async_copy(grad_out, g_v, w_sem.at[2])
    load_q = pltpu.make_async_copy(queries.at[:, mine_k], q_v.at[0], w_sem.at[3])
    load_o = pltpu.make_async_copy(queries.at[:, other_k], q_o, w_sem.at[4])

    def load_step(step):
        s, ks = STEPS[step]
        for n, k in enumerate(ks):
            rows = pl.ds(pl.multiple_of(flip(t, k, 3) * 256 + s * SEQ, SEQ), SEQ)
            pltpu.make_async_copy(hidden.at[rows], x_v.at[FIRST[step] + n], x_sem.at[step]).start()

    load_q.start()
    load_o.start()
    load_wi.start()
    load_step(0)

    with jax.named_scope("greet"):
        barrier = pltpu.get_barrier_semaphore()
        greeted = [tc_peer(0, *o) for o in SLOTS[:0:-1]]
        greeted += [at(*ahead(0, dz)) for dz in (2, 6, 1, 7)] + [at(*ahead(2, 0))]
        greeted += [at(lax.rem(x + 3 + 2 * xl, 4), z), tc_peer(1, 0, 0)]
        for peer in greeted:
            tell(barrier, peer)

    for step in range(1, len(STEPS)):
        load_step(step)
    load_wo.start()
    load_g.start()

    with jax.named_scope("entry_wait"):
        pl.semaphore_wait(barrier, len(greeted))

    with jax.named_scope("heard_0"):
        for dz in (2, 6, 1, 7):
            tell(wave.at[1], at(*ahead(0, dz)))
        tell(wave.at[0], tc_peer(1, 0, 0))

    with jax.named_scope("query_send"):
        load_q.wait()
        load_o.wait()
        remote(q_v.at[0], q_v.at[8], qc_ss, qc_rs, tc_peer(1, 0, 0)).start()
        remote(q_o, q_v.at[1], q_ss, q_rs.at[0], tc_peer(0, 0, 1)).start()
        remote(q_v.at[0], q_v.at[3], q_ss, q_rs.at[1], tc_peer(0, 1, 0)).start()
        remote(q_v.at[0], q_v.at[2], q_ss, q_rs.at[1], tc_peer(0, 3, 0)).start()

    own = {}

    def project(step):
        s, ks = STEPS[step]
        rows = pl.ds(FIRST[step], len(ks))
        settle(x_v.at[rows], x_sem.at[step])
        parts = dot_nt(wi_v[...], x_v[rows].reshape(len(ks) * SEQ, FF_PART))
        for n, k in enumerate(ks):
            part = parts[:, n * SEQ : (n + 1) * SEQ]
            if k:
                rs_send[s, k] = part.astype(BF16)
            else:
                own[s] = part

    def send_parts(step):
        s, ks = STEPS[step]
        for k in ks:
            if k:
                remote(rs_send.at[s, k], rs_recv.at[s, k], rs_ss, rs_rs.at[s], t_peer(k)).start()

    load_wi.wait()
    with jax.named_scope("hidden_0"):
        project(0)
        send_parts(0)
    with jax.named_scope("hidden_1"):
        project(1)
        send_parts(1)
    with jax.named_scope("hidden_2"):
        project(2)
        send_parts(2)
    with jax.named_scope("heard_1"):
        pl.semaphore_wait(wave.at[1], 4)
        for dz in (4, 3, 5):
            tell(wave.at[2], at(*ahead(0, dz)))
    with jax.named_scope("hidden_3"):
        project(3)
        send_parts(3)
    with jax.named_scope("hidden_4"):
        project(4)
        send_parts(4)

    with jax.named_scope("grad_part"):
        load_wo.wait()
        load_g.wait()
        pout = dot_nt(wo_v[...], g_v[...]).astype(BF16)

    with jax.named_scope("heard_2"):
        pl.semaphore_wait(wave.at[0], 1)
        pl.semaphore_wait(wave.at[2], 3)

    def features(s):
        with jax.named_scope("part_wait_%d" % s):
            settle(rs_recv.at[s, pl.ds(1, 7)], rs_rs.at[s])
        with jax.named_scope("outer"):
            pin = own[s]
            for k in range(1, 8):
                pin = pin + rs_recv[s, k].astype(F32)
            hi = pin.astype(BF16)
            lo = (pin - hi.astype(F32)).astype(BF16)
            right = pout[:, s * SEQ : (s + 1) * SEQ]
            twice = jnp.concatenate([right, right], axis=0)
            r_v[:RANK] = (dot_nt(hi, twice) + dot_nt(lo, twice)) * (SEQ ** -0.5)
            left = lax.broadcasted_iota(jnp.int32, (RANK // 2, LANES), 1) < RANK
            even, odd = r_v[pl.ds(0, 32, stride=2), :], r_v[pl.ds(1, 32, stride=2), :]
            f = jnp.where(left, even, odd).astype(BF16)
            f_send[s, 0] = f[:TILES]
            f_send[s, 1] = f[TILES:]
        with jax.named_scope("feature_send_%d" % s):
            for n, (dx, dz) in enumerate(xz_all):
                src = f_send.at[s, lax.rem(xl + dx, 2)]
                remote(src, f_recv.at[s, n], f_ss, f_rs, at(*ahead(dx, dz))).start()

    with jax.named_scope("query_2"):
        settle(q_v.at[1], q_rs.at[0])
        remote(q_v.at[1], q_v.at[5], q_ss, q_rs.at[2], tc_peer(0, 1, 0)).start()
        remote(q_v.at[1], q_v.at[4], q_ss, q_rs.at[2], tc_peer(0, 3, 0)).start()
    features(0)
    features(1)
    with jax.named_scope("query_3"):
        first, last = pl.ds(0, HALF_K // 2), pl.ds(HALF_K // 2, HALF_K // 2)
        for kx in range(2):
            settle(q_v.at[pl.ds(2 + 2 * kx, 2)], q_rs.at[1 + kx])
            for slot, part, dy in ((3, first, 1), (2, last, 3)):
                remote(
                    q_v.at[slot + 2 * kx, :, part], q_v.at[6 + kx, :, part], q_ss, q_rs.at[3],
                    tc_peer(0, dy, 0),
                ).start()
        remote(q_v.at[pl.ds(1, 5)], q_v.at[pl.ds(9, 5)], qc_ss, qc_rs, tc_peer(1, 0, 0)).start()

    with jax.named_scope("places"):
        row = lax.broadcasted_iota(jnp.int32, (512, LANES), 0)
        lane = lax.broadcasted_iota(jnp.int32, (512, LANES), 1)
        b_, dy_ = row // 256, (row // 64) % 4
        x_, z_, s_ = (row // 16) % 4, (row // 2) % 8, row % 2
        src_c = (c + b_) % 2
        src_t = ((y + dy_) % 4) * 2 + x_ % 2
        target = (((x_ // 2) * 8 + z_) * 2 + src_c) * 16 + src_t * 2 + s_
        for block in range(4):
            perm[:, block * LANES : (block + 1) * LANES] = jnp.where(
                target == lane + block * LANES, 1.0, 0.0
            ).astype(BF16)

    with jax.named_scope("query_core"):
        settle(q_v.at[pl.ds(6, 2)], q_rs.at[3])
        remote(q_v.at[pl.ds(6, 2)], q_v.at[pl.ds(14, 2)], qc_ss, qc_rs, tc_peer(1, 0, 0)).start()

    def spread(px, pz, s, block):
        feats[pl.ds((px * 8 + pz) * 2 + s, TILES, stride=PITCH), :] = block.astype(F32)

    with jax.named_scope("feature_wait"):
        settle(f_recv, f_rs)
    with jax.named_scope("spread"):
        for s in range(2):
            spread(x, z, s, f_send[s, xl])
            for n, (dx, dz) in enumerate(xz_all):
                spread(*behind(dx, dz), s, f_recv[s, n])
    with jax.named_scope("query_wait"):
        settle(q_v.at[pl.ds(8, 8)], qc_rs)

    with jax.named_scope("score_dot"):
        right = jnp.concatenate(
            [feats[i * PITCH : i * PITCH + 64, :].astype(BF16) for i in range(TILES)], axis=1
        )

    for first in (4, 0):
        with jax.named_scope("score_part"):
            rows = jnp.concatenate([q_v[first : first + 4], q_v[first + 8 : first + 12]], axis=0)
            scores = dot_nt(rows.reshape(128, HALF_K), right) * (1.0 / RANK)
            scores = scores.reshape(8, 2, 8, 64)
            packed = jnp.concatenate([scores[:, 0], scores[:, 1]], axis=2)
            s_send[first : first + 4] = packed[:4]
            s_send[first + 8 : first + 12] = packed[4:]
        with jax.named_scope("score_send"):
            for b, dy, kx in tc_all:
                n = SLOTS.index((dy, kx))
                there = b * 8 + SLOTS.index(((4 - dy) % 4, kx))
                if first <= n < first + 4:
                    remote(
                        s_send.at[b * 8 + n], s_recv.at[there], s_ss, s_rs, tc_peer(b, dy, kx)
                    ).start()

    with jax.named_scope("score_wait"):
        settle(s_recv.at[pl.ds(1, 15)], s_rs)
    with jax.named_scope("place"):
        left = lax.broadcasted_iota(jnp.int32, (8, LANES), 1) < 64
        upper, lower = [], []
        for g in range(4):
            pair = []
            for dy in range(2 * (g % 2), 2 * (g % 2) + 2):
                one, two = [(g // 2) * 8 + SLOTS.index((dy, kx)) for kx in range(2)]
                pair.append((s_recv[one] if one else s_send[0]) + s_recv[two])
            upper.append(jnp.where(left, pair[0], pltpu.roll(pair[1], 64, 1)))
            lower.append(jnp.where(left, pltpu.roll(pair[0], 64, 1), pair[1]))
        wide = jnp.concatenate(
            [jnp.concatenate(upper, axis=1), jnp.concatenate(lower, axis=1)], axis=0
        )
        p1 = wide.astype(BF16)
        rest = wide - p1.astype(F32)
        p2 = rest.astype(BF16)
        p3 = (rest - p2.astype(F32)).astype(BF16)
        placed = dot_nn(jnp.concatenate([p1, p2, p3], axis=0), perm[...])
        out[...] = (placed[:16] + placed[16:32]) + placed[32:]

    with jax.named_scope("send_wait"):
        settle(rs_send.at[:, pl.ds(1, 7)], rs_ss)
        settle(q_v.at[pl.ds(0, 7)], q_ss)
        settle(q_v.at[pl.ds(0, 8)], qc_ss)
        settle(f_recv, f_ss)
        settle(s_send.at[pl.ds(1, 15)], s_ss)


def body(hidden, grad_out, proj_in, proj_out, queries):
    dma = pltpu.SemaphoreType.DMA
    scratch = [
        pltpu.VMEM((16, SEQ, FF_PART), BF16),
        pltpu.VMEM((256, D), BF16),
        pltpu.VMEM((RANK, FF_PART), BF16),
        pltpu.VMEM((RANK, D), BF16),
        pltpu.VMEM((16, 16, HALF_K), BF16),
        pltpu.VMEM((16, HALF_K), BF16),
        pltpu.VMEM((2, 8, RANK, SEQ), BF16),
        pltpu.VMEM((2, 8, RANK, SEQ), BF16),
        pltpu.VMEM((RANK + 8, LANES), F32),
        pltpu.VMEM((2, 2, TILES, LANES), BF16),
        pltpu.VMEM((2, 31, TILES, LANES), BF16),
        pltpu.VMEM(((TILES + 1) * PITCH, LANES), F32),
        pltpu.VMEM((16, 8, LANES), F32),
        pltpu.VMEM((16, 8, LANES), F32),
        pltpu.VMEM((512, 512), BF16),
        dma((5,)), dma((5,)), dma, dma((2,)), dma, dma((4,)), *[dma] * 6,
        pltpu.SemaphoreType.REGULAR((3,)),
    ]
    return pl.pallas_call(
        kernel,
        out_shape=jax.ShapeDtypeStruct((16, 512), F32),
        in_specs=[pl.BlockSpec(memory_space=pltpu.HBM)] * 5,
        out_specs=pl.BlockSpec(memory_space=pltpu.VMEM),
        scratch_shapes=scratch,
        compiler_params=pltpu.CompilerParams(
            collective_id=0, has_side_effects=True, vmem_limit_bytes=56418304
        ),
    )(hidden, grad_out, proj_in, proj_out, queries)


def solution(mesh):
    placed = (
        P("dp", "tensor"),
        P(("dp", "tensor"), None),
        P(None, "tensor"),
        P(),
        P(("dp", "tensor"), None),
    )
    return jax.shard_map(
        body, mesh=mesh, in_specs=placed, out_specs=P(("dp", "tensor"), None), check_vma=False
    )
```
